32 devices in a mesh: groups: 2 (over y), row: 4 (over z), chan: 2 (over x), sub: 2 (over core).
Axes of the slice: x: 2, y: 2, z: 4, core: 2. Of those that a mesh axis runs over, the one named last changes fastest.
Arguments:
- pair: bfloat16 [384, 192, 128], P(('groups', 'row'), ('chan', 'sub')), parts along dimension 0, may hold values from -6 to 6
- chain_len: int32 [8], P('groups'), parts along dimension 0, may hold values from 1 to 48, 144 in all
- norm_gain: float32 [128], replicated, may hold values from 0.1 to 1.9
- norm_bias: float32 [128], replicated, may hold values from -3 to 3
- left_proj: bfloat16 [128, 128], replicated, may hold values from -0.5 to 0.5
- left_gate: bfloat16 [128, 128], replicated, may hold values from -0.5 to 0.5
- right_proj: bfloat16 [128, 128], replicated, may hold values from -0.5 to 0.5
- right_gate: bfloat16 [128, 128], replicated, may hold values from -0.5 to 0.5
- out_norm_gain: float32 [128], replicated, may hold values from 0.1 to 1.9
- out_norm_bias: float32 [128], replicated, may hold values from -3 to 3
- out_proj: bfloat16 [128, 128], replicated, may hold values from -0.5 to 0.5
- out_gate: bfloat16 [128, 128], replicated, may hold values from -0.5 to 0.5
Outputs:
- relaid: bfloat16 [384, 192, 128], P('groups', ('chan', 'sub', 'row')), parts along dimension 0
The draws below stay inside these ranges and needn't reach their ends.
There are 2 independent parts, one for each index of `groups`. The reference program is written for one: setup_inputs(seed, part) draws one part's arguments, and reference() takes and returns one part's arrays. A program takes and returns all parts, laid end to end along the dimension named above; an argument that names none is the same for every part. Nothing has to cross between parts.
Inputs may be any that keep to these rules, and one draw needn't show every extreme that they name: Chain c occupies residues c * (48) onward; its first chain_len[c] residues are valid. The entries sum to 144 and one of them equals 48.
All inputs are finite; a program needn't handle non-finite values.
Results may differ from the reference program's by a relative error of at most 0.0038.
Values may be sent and summed in bfloat16 or wider, within the bound.
A program may use at most 64 MiB of HBM per device.

```python
import math
import jax
import jax.numpy as jnp
import numpy as np
from jax import lax

C = 128
HID = 128
CHAINS = 4
N = 192


def block_levels(own_key, extent, shards, least, largest):
    level = 1.0
    for dim, shards_of in shards:
        heights = jax.random.uniform(jax.random.fold_in(jax.random.fold_in(own_key, 6), dim), (shards_of,), jnp.float32, least / len(shards), largest / len(shards))
        level = level * jnp.repeat(jnp.exp(heights), extent[dim] // shards_of).reshape((-1,) + (1,) * (len(extent) - 1 - dim))
    return level


def length_profile(amount, total, reach, skew):
    loads = [(1 << 20) // math.isqrt(rank ** skew) + 1 for rank in range(2, amount + 1)]
    spare, holding = total - reach - (amount - 1), [1] * (amount - 1)
    while spare > 0:
        candidates = [i for i in range(amount - 1) if holding[i] < reach]
        mass, budget = sum([loads[i] for i in candidates]), spare
        for i in candidates:
            extra = min(reach - holding[i], max(1, budget * loads[i] // mass), spare)
            holding[i] = holding[i] + extra
            spare = spare - extra
    return np.array([reach] + holding)


def ragged(key, amount, total, most, slope):
    if amount == 2:
        one = jax.random.randint(key, (), max(1, total - most), min(most, total - 1) + 1)
        return jnp.stack([one, total - one])
    sizes = jnp.asarray(length_profile(amount, total, most, slope), jnp.int32)
    couples = (amount - 1) // 2
    donor, sink = sizes[1:1 + 2 * couples:2], sizes[2:2 + 2 * couples:2]
    slack = jnp.minimum(donor - 1, most - sink)
    shifted = jax.random.randint(jax.random.fold_in(key, 1), (couples,), 0, 1 << 20) % (slack + 1)
    sizes = sizes.at[1:1 + 2 * couples:2].set(donor - shifted).at[2:2 + 2 * couples:2].set(sink + shifted)
    return sizes[jax.random.permutation(jax.random.fold_in(key, 2), amount)]


def scatter_about(stream_key, extent, width, most, cuts=(), held_as=jnp.bfloat16):
    values = jax.random.normal(stream_key, extent, jnp.float32) * width
    if len(cuts) > 0:
        values = block_levels(stream_key, extent, cuts, -0.22, 0.18) * values
    return jnp.clip(values, min=-most, max=most).astype(held_as)


def setup_inputs(seed: int = 0, part: int = 0) -> dict:
    key_of = jax.random.split(jax.random.key(seed), 13)
    own_keys = jax.random.split(jax.random.fold_in(key_of[12], part), 13)
    pair = scatter_about(own_keys[0], (N, N, C), 1.0, 6.0, ((0, 4), (1, 4)))
    chain_len = ragged(own_keys[1], CHAINS, 3 * N // 4, N // CHAINS, 1).astype(jnp.int32)
    norm_gain = jnp.clip(1.0 + 0.18 * jax.random.normal(key_of[2], (C,), jnp.float32), 0.1, 1.9)
    norm_bias = scatter_about(key_of[3], (C,), 0.5, 3.0, (), jnp.float32)
    left_proj = scatter_about(key_of[4], (C, HID), C ** -0.5, 0.5)
    left_gate = scatter_about(key_of[5], (C, HID), C ** -0.5, 0.5)
    right_proj = scatter_about(key_of[6], (C, HID), C ** -0.5, 0.5)
    right_gate = scatter_about(key_of[7], (C, HID), C ** -0.5, 0.5)
    out_norm_gain = jnp.clip(1.0 + 0.18 * jax.random.normal(key_of[8], (HID,), jnp.float32), 0.1, 1.9)
    out_norm_bias = scatter_about(key_of[9], (HID,), 0.5, 3.0, (), jnp.float32)
    out_proj = scatter_about(key_of[10], (HID, C), HID ** -0.5, 0.5)
    out_gate = scatter_about(key_of[11], (C, C), C ** -0.5, 0.5)
    return dict(pair=pair, chain_len=chain_len, norm_gain=norm_gain, norm_bias=norm_bias, left_proj=left_proj, left_gate=left_gate, right_proj=right_proj, right_gate=right_gate, out_norm_gain=out_norm_gain, out_norm_bias=out_norm_bias, out_proj=out_proj, out_gate=out_gate)


EPS = 1e-05

def layer_norm(values, gain, bias, axis):
    mean = lax.optimization_barrier(jnp.mean(values, axis=axis, keepdims=True))
    centred = values - mean
    spread = lax.optimization_barrier(jnp.mean(centred * centred, axis=axis, keepdims=True))
    return centred * lax.rsqrt(spread + EPS) * gain + bias

def residue_valid(positions, chain_len, slot):
    owner = positions // slot
    picks = owner[:, None] == jnp.arange(chain_len.shape[0], dtype=jnp.int32)[None, :]
    limit = lax.optimization_barrier(jnp.sum(jnp.where(picks, chain_len[None, :], 0), axis=1))
    return (positions % slot < limit).astype(jnp.float32)

def reference(pair, chain_len, norm_gain, norm_bias, left_proj, left_gate, right_proj, right_gate, out_norm_gain, out_norm_bias, out_proj, out_gate):
    total = pair.shape[0]
    positions = jnp.arange(total, dtype=jnp.int32)
    valid = residue_valid(positions, chain_len, total // CHAINS)
    block = math.gcd(total, 32)
    count = total // block
    pair_blocks = pair.reshape(count, block, total, C)

    def sides(items):
        rows, row_valid = items
        normed = layer_norm(rows.astype(jnp.float32), norm_gain, norm_bias, -1).astype(jnp.bfloat16)
        flat = normed.reshape(-1, C)

        def project(weights):
            return jnp.dot(flat, weights, preferred_element_type=jnp.float32).reshape(block, total, HID)
        weight = row_valid[:, None, None] * valid[None, :, None]
        left = (weight * jax.nn.sigmoid(project(left_gate)) * project(left_proj)).astype(jnp.bfloat16)
        right = (weight * jax.nn.sigmoid(project(right_gate)) * project(right_proj)).astype(jnp.bfloat16)
        return (left, right)
    left, right = lax.map(sides, (pair_blocks, valid.reshape(count, block)))
    left_chan = jnp.transpose(left.reshape(total, total, HID), (2, 0, 1))
    right_chan = jnp.transpose(right.reshape(total, total, HID), (2, 0, 1))

    def channel(items):
        first, second = items
        return jnp.dot(first, second.T, preferred_element_type=jnp.float32).astype(jnp.bfloat16)
    tri = lax.map(channel, (left_chan, right_chan))
    tri = jnp.transpose(tri, (1, 2, 0)).reshape(count, block, total, HID)

    def finish(items):
        rows, tri_rows = items
        normed = layer_norm(rows.astype(jnp.float32), norm_gain, norm_bias, -1).astype(jnp.bfloat16).reshape(-1, C)
        gate = jax.nn.sigmoid(jnp.dot(normed, out_gate, preferred_element_type=jnp.float32))
        tri_normed = layer_norm(tri_rows.astype(jnp.float32), out_norm_gain, out_norm_bias, -1).astype(jnp.bfloat16).reshape(-1, HID)
        update = jnp.dot(tri_normed, out_proj, preferred_element_type=jnp.float32)
        result = rows.reshape(-1, C).astype(jnp.float32) + gate * update
        return result.astype(jnp.bfloat16).reshape(rows.shape)
    relaid = lax.map(finish, (pair_blocks, tri))
    return relaid.reshape(total, total, C)
```

```python
import functools

import jax
import jax.numpy as jnp
from jax import lax
from jax.experimental import pallas as pl
from jax.experimental.pallas import tpu as pltpu
from jax.sharding import PartitionSpec as P

EPS = 1e-05


def layer_norm(values, gain, bias, axis):
    mean = jnp.mean(values, axis=axis, keepdims=True)
    centred = values - mean
    spread = jnp.mean(centred * centred, axis=axis, keepdims=True)
    return centred * lax.rsqrt(spread + EPS) * gain + bias


def residue_valid(positions, chain_len, slot):
    owner = positions // slot
    picks = owner[:, None] == jnp.arange(chain_len.shape[0], dtype=jnp.int32)[None, :]
    limit = jnp.sum(jnp.where(picks, chain_len[None, :], 0), axis=1)
    return (positions % slot < limit).astype(jnp.float32)


def finish(base_flat, base_normed, tri_flat, out_norm_gain, out_norm_bias, out_proj, out_gate):
    gate = jax.nn.sigmoid(jnp.dot(base_normed, out_gate, preferred_element_type=jnp.float32))
    tri_normed = layer_norm(
        tri_flat.astype(jnp.float32), out_norm_gain[:, None], out_norm_bias[:, None], 0
    ).astype(jnp.bfloat16)
    update = jnp.einsum("hp,hc->pc", tri_normed, out_proj, preferred_element_type=jnp.float32)
    return (base_flat.astype(jnp.float32) + gate * update).astype(jnp.bfloat16)


def shards_general(
    pair,
    chain_len,
    norm_gain,
    norm_bias,
    left_proj,
    left_gate,
    right_proj,
    right_gate,
    out_norm_gain,
    out_norm_bias,
    out_proj,
    out_gate,
):
    rows, width, chans = pair.shape
    hidden = left_proj.shape[1]
    row_count = lax.axis_size("row")
    total = rows * row_count
    slot = total // chain_len.shape[0]
    column_block = lax.axis_index("chan") * lax.axis_size("sub") + lax.axis_index("sub")
    row_ids = lax.axis_index("row") * rows + jnp.arange(rows, dtype=jnp.int32)
    col_ids = column_block * width + jnp.arange(width, dtype=jnp.int32)
    row_valid = residue_valid(row_ids, chain_len, slot)
    col_valid = residue_valid(col_ids, chain_len, slot)
    flat = pair.reshape(rows * width, chans)
    normed = layer_norm(flat.astype(jnp.float32), norm_gain, norm_bias, 1).astype(jnp.bfloat16)
    w_in = jnp.concatenate([left_proj, left_gate, right_proj, right_gate], axis=1)
    projected = jnp.einsum("pc,cf->fp", normed, w_in, preferred_element_type=jnp.float32)
    weight = (row_valid[:, None] * col_valid[None, :]).reshape(1, rows * width)
    left_t = (
        (weight * jax.nn.sigmoid(projected[hidden : 2 * hidden]) * projected[:hidden])
        .astype(jnp.bfloat16)
        .reshape(hidden, rows, width)
    )
    right_t = (
        (weight * jax.nn.sigmoid(projected[3 * hidden :]) * projected[2 * hidden : 3 * hidden])
        .astype(jnp.bfloat16)
        .reshape(hidden, rows, width)
    )
    left_c, right_c = (
        lax.all_to_all(left_t, ("chan", "sub"), split_axis=0, concat_axis=2, tiled=True),
        lax.all_to_all(right_t, ("chan", "sub"), split_axis=0, concat_axis=2, tiled=True),
    )
    tri = jnp.einsum(
        "cik,cjk->cij",
        left_c,
        lax.all_gather(right_c, "row", axis=1, tiled=True),
        preferred_element_type=jnp.float32,
    ).astype(jnp.bfloat16)
    back = lax.all_to_all(tri, ("chan", "sub"), split_axis=2, concat_axis=0, tiled=True)
    tri_flat = back.reshape(hidden, rows * width)
    result = finish(flat, normed, tri_flat, out_norm_gain, out_norm_bias, out_proj, out_gate)
    relaid = lax.all_to_all(
        result.reshape(rows, width, chans), "row", split_axis=1, concat_axis=0, tiled=True
    )
    return relaid


MESH = pl.DeviceIdType.MESH


def place(rows, chans, subs):
    row, chan, sub = lax.axis_index("row"), lax.axis_index("chan"), lax.axis_index("sub")
    return (row * chans + chan) * subs + sub


def coords(member, chans, subs):
    return {
        "row": member // (chans * subs),
        "chan": (member // subs) % chans,
        "sub": member % subs,
    }


def greet(me, count, chans, subs):
    barrier = pltpu.get_barrier_semaphore()
    for step in range(1, count):
        peer = lax.rem(me + step, count)
        pl.semaphore_signal(
            barrier, inc=1, device_id=coords(peer, chans, subs), device_id_type=MESH
        )
    pl.semaphore_wait(barrier, count - 1)


def norm_rows(values, gain, bias):
    mean = jnp.mean(values, axis=1, keepdims=True)
    centred = values - mean
    spread = jnp.mean(centred * centred, axis=1, keepdims=True)
    return centred * lax.rsqrt(spread + EPS) * gain + bias


def norm_columns(values, gain, bias):
    mean = jnp.mean(values, axis=0, keepdims=True)
    centred = values - mean
    spread = jnp.mean(centred * centred, axis=0, keepdims=True)
    return centred * lax.rsqrt(spread + EPS) * gain + bias


def sides_kernel(
    dims, step_columns, pair, weight, gain, bias, w_in, got, moved, out, w_t, sems, pair_sems, own_sems
):
    rows, chans, subs = dims
    count = rows * chans * subs
    me = place(rows, chans, subs)
    greet(me, count, chans, subs)
    width, height, depth = pair.shape
    share = width // rows
    my_row = lax.axis_index("row")
    pending = []
    own_pair = pltpu.make_async_copy(
        pair.at[pl.ds(my_row * share, share)],
        moved.at[:, pl.ds(pl.multiple_of(my_row * height, height), height)],
        own_sems.at[0],
    )
    own_pair.start()
    pending.append(own_pair)
    for step in range(1, rows):
        target = lax.rem(my_row + step, rows)
        copy = pltpu.make_async_remote_copy(
            src_ref=pair.at[pl.ds(target * share, share)],
            dst_ref=moved.at[:, pl.ds(pl.multiple_of(my_row * height, height), height)],
            send_sem=pair_sems.at[0, step],
            recv_sem=pair_sems.at[1, step],
            device_id={"row": target},
            device_id_type=MESH,
        )
        copy.start()
        pending.append(copy)
    hidden = w_in.shape[1] // 4
    w_t[...] = w_in[...].astype(jnp.float32).T.astype(jnp.bfloat16)
    lanes = step_columns * height
    per = hidden // count

    def body(index, carry):
        block = pair[pl.ds(index * step_columns, step_columns)]
        flat = block.astype(jnp.float32).reshape(lanes, depth)
        normed = norm_rows(flat, gain[...], bias[...]).astype(jnp.bfloat16)
        projected = lax.dot_general(
            w_t[...], normed, (((1,), (1,)), ((), ())), preferred_element_type=jnp.float32
        )
        span = pl.ds(pl.multiple_of(index * lanes, 128), lanes)
        valid = weight[:, span]
        left = valid * jax.nn.sigmoid(projected[hidden : 2 * hidden]) * projected[:hidden]
        right = (
            valid * jax.nn.sigmoid(projected[3 * hidden :]) * projected[2 * hidden : 3 * hidden]
        )
        both = jnp.concatenate(
            [left.reshape(count, per, lanes), right.reshape(count, per, lanes)], axis=1
        )
        out[:, :, span] = both.astype(jnp.bfloat16)
        return carry

    lax.fori_loop(0, width // step_columns, body, 0)
    own = pltpu.make_async_copy(out.at[me], got.at[me], own_sems.at[1])
    own.start()
    pending.append(own)
    for step in range(1, count):
        peer = lax.rem(me + step, count)
        copy = pltpu.make_async_remote_copy(
            src_ref=out.at[peer],
            dst_ref=got.at[me],
            send_sem=sems.at[0, step],
            recv_sem=sems.at[1, step],
            device_id=coords(peer, chans, subs),
            device_id_type=MESH,
        )
        copy.start()
        pending.append(copy)
    for copy in pending:
        copy.wait()


def finish_kernel(
    dims, step_lanes, out, moved, gain, bias, out_gain, out_bias, proj, gate_w, result, got, sems, own_sem
):
    rows, chans, subs = dims
    count = rows * chans * subs
    me = place(rows, chans, subs)
    greet(me, count, chans, subs)

    def block_of(member):
        return (member % (chans * subs)) * rows + member // (chans * subs)

    own = pltpu.make_async_copy(out.at[block_of(me)], got.at[me], own_sem)
    own.start()
    pending = [own]
    for step in range(1, count):
        peer = lax.rem(me + step, count)
        copy = pltpu.make_async_remote_copy(
            src_ref=out.at[block_of(peer)],
            dst_ref=got.at[me],
            send_sem=sems.at[0, step],
            recv_sem=sems.at[1, step],
            device_id=coords(peer, chans, subs),
            device_id_type=MESH,
        )
        copy.start()
        pending.append(copy)
    for copy in pending:
        copy.wait()
    half = got.shape[2]
    per = got.shape[1] // 2
    depth = moved.shape[1]

    def body(index, carry):
        lanes = pl.ds(pl.multiple_of(index * step_lanes, 128), step_lanes)
        tri = got[:, :, lanes].astype(jnp.float32)
        for part in range(2):
            piece = tri[:, part * per : (part + 1) * per].reshape(count * per, step_lanes)
            tri_normed = norm_columns(piece, out_gain[...], out_bias[...]).T.astype(jnp.bfloat16)
            update = jnp.dot(tri_normed, proj[...], preferred_element_type=jnp.float32)
            span = pl.ds(pl.multiple_of(part * half + index * step_lanes, 128), step_lanes)
            base = moved[span, :].astype(jnp.float32)
            normed = norm_rows(base, gain[...], bias[...]).astype(jnp.bfloat16)
            gate = jax.nn.sigmoid(jnp.dot(normed, gate_w[...], preferred_element_type=jnp.float32))
            result[span, :] = (base + gate * update).astype(jnp.bfloat16)
        return carry

    lax.fori_loop(0, half // step_lanes, body, 0)


def product(got, dims, per, width, height):
    rows, chans, subs = dims
    blocks = chans * subs
    sides = got.reshape(rows, blocks, 2, per, width, height)
    sides = sides.transpose(2, 3, 1, 4, 0, 5).reshape(2, per, blocks * width, rows * height)
    tri = jnp.einsum(
        "ckj,cki->cji", sides[1], sides[0], preferred_element_type=jnp.float32
    ).astype(jnp.bfloat16)
    count = rows * blocks
    total = rows * height
    share = total // count
    tri = tri.reshape(per, count, 2, share // 2, total).transpose(1, 2, 0, 3, 4)
    return tri.reshape(count, 2 * per, share // 2 * total)


def shards_direct(
    pair,
    chain_len,
    norm_gain,
    norm_bias,
    left_proj,
    left_gate,
    right_proj,
    right_gate,
    out_norm_gain,
    out_norm_bias,
    out_proj,
    out_gate,
):
    height, width, depth = pair.shape
    hidden = left_proj.shape[1]
    dims = (lax.axis_size("row"), lax.axis_size("chan"), lax.axis_size("sub"))
    count = dims[0] * dims[1] * dims[2]
    per = hidden // count
    total = height * dims[0]
    slot = total // chain_len.shape[0]
    column_block = lax.axis_index("chan") * lax.axis_size("sub") + lax.axis_index("sub")
    row_ids = lax.axis_index("row") * height + jnp.arange(height, dtype=jnp.int32)
    col_ids = column_block * width + jnp.arange(width, dtype=jnp.int32)
    row_valid = residue_valid(row_ids, chain_len, slot)
    col_valid = residue_valid(col_ids, chain_len, slot)
    weight = (col_valid[:, None] * row_valid[None, :]).reshape(1, width * height)
    turned = pair.transpose(1, 0, 2)
    w_in = jnp.concatenate([left_proj, left_gate, right_proj, right_gate], axis=1)
    whole = pl.BlockSpec(memory_space=pltpu.VMEM)
    share = width // dims[0]
    got, moved = pl.pallas_call(
        functools.partial(sides_kernel, dims, 8),
        out_shape=(
            jax.ShapeDtypeStruct((count, 2 * per, width * height), jnp.bfloat16),
            jax.ShapeDtypeStruct((share, total, depth), jnp.bfloat16),
        ),
        in_specs=[whole] * 5,
        out_specs=(whole, whole),
        scratch_shapes=[
            pltpu.VMEM((count, 2 * per, width * height), jnp.bfloat16),
            pltpu.VMEM((4 * hidden, depth), jnp.bfloat16),
            pltpu.SemaphoreType.DMA((2, count)),
            pltpu.SemaphoreType.DMA((2, dims[0])),
            pltpu.SemaphoreType.DMA((2,)),
        ],
        compiler_params=pltpu.CompilerParams(
            collective_id=0, has_side_effects=True, vmem_limit_bytes=32 << 20
        ),
        name="sides",
    )(turned, weight, norm_gain[None, :], norm_bias[None, :], w_in)
    tri = product(got, dims, per, width, height)
    half = share * total // 2
    result = pl.pallas_call(
        functools.partial(finish_kernel, dims, 384),
        out_shape=jax.ShapeDtypeStruct((share * total, depth), jnp.bfloat16),
        in_specs=[whole] * 8,
        out_specs=whole,
        scratch_shapes=[
            pltpu.VMEM((count, 2 * per, half), jnp.bfloat16),
            pltpu.SemaphoreType.DMA((2, count)),
            pltpu.SemaphoreType.DMA,
        ],
        compiler_params=pltpu.CompilerParams(
            collective_id=1, has_side_effects=True, vmem_limit_bytes=32 << 20
        ),
        name="finish",
    )(
        tri,
        moved.reshape(share * total, depth),
        norm_gain[None, :],
        norm_bias[None, :],
        out_norm_gain[:, None],
        out_norm_bias[:, None],
        out_proj,
        out_gate,
    )
    return result.reshape(share, total, depth).transpose(1, 0, 2)


def shards(pair, chain_len, *params):
    height, width, _ = pair.shape
    hidden = params[2].shape[1]
    rows = lax.axis_size("row")
    count = rows * lax.axis_size("chan") * lax.axis_size("sub")
    fits = (
        count * 8 == hidden
        and height % 16 == 0
        and width % (2 * rows) == 0
        and (8 * height) % 128 == 0
        and width % 8 == 0
        and (width // rows * height * rows) % 768 == 0
    )
    body = shards_direct if fits else shards_general
    return body(pair, chain_len, *params)


def solution(mesh):
    return jax.shard_map(
        shards,
        mesh=mesh,
        in_specs=(
            P(("groups", "row"), ("chan", "sub"), None),
            P("groups"),
            P(),
            P(),
            P(),
            P(),
            P(),
            P(),
            P(),
            P(),
            P(),
            P(),
        ),
        out_specs=P("groups", ("chan", "sub", "row"), None),
        check_vma=False,
    )
```

```python
import functools

import jax
import jax.numpy as jnp
from jax import lax
from jax.experimental import pallas as pl
from jax.experimental.pallas import tpu as pltpu
from jax.sharding import PartitionSpec as P

EPS = 1e-05


def layer_norm(values, gain, bias, axis):
    mean = jnp.mean(values, axis=axis, keepdims=True)
    centred = values - mean
    spread = jnp.mean(centred * centred, axis=axis, keepdims=True)
    return centred * lax.rsqrt(spread + EPS) * gain + bias


def residue_valid(positions, chain_len, slot):
    owner = positions // slot
    picks = owner[:, None] == jnp.arange(chain_len.shape[0], dtype=jnp.int32)[None, :]
    limit = jnp.sum(jnp.where(picks, chain_len[None, :], 0), axis=1)
    return (positions % slot < limit).astype(jnp.float32)


def finish(base_flat, base_normed, tri_flat, out_norm_gain, out_norm_bias, out_proj, out_gate):
    gate = jax.nn.sigmoid(jnp.dot(base_normed, out_gate, preferred_element_type=jnp.float32))
    tri_normed = layer_norm(
        tri_flat.astype(jnp.float32), out_norm_gain[:, None], out_norm_bias[:, None], 0
    ).astype(jnp.bfloat16)
    update = jnp.einsum("hp,hc->pc", tri_normed, out_proj, preferred_element_type=jnp.float32)
    return (base_flat.astype(jnp.float32) + gate * update).astype(jnp.bfloat16)


def shards_general(
    pair,
    chain_len,
    norm_gain,
    norm_bias,
    left_proj,
    left_gate,
    right_proj,
    right_gate,
    out_norm_gain,
    out_norm_bias,
    out_proj,
    out_gate,
):
    rows, width, chans = pair.shape
    hidden = left_proj.shape[1]
    row_count = lax.axis_size("row")
    total = rows * row_count
    slot = total // chain_len.shape[0]
    column_block = lax.axis_index("chan") * lax.axis_size("sub") + lax.axis_index("sub")
    row_ids = lax.axis_index("row") * rows + jnp.arange(rows, dtype=jnp.int32)
    col_ids = column_block * width + jnp.arange(width, dtype=jnp.int32)
    row_valid = residue_valid(row_ids, chain_len, slot)
    col_valid = residue_valid(col_ids, chain_len, slot)
    flat = pair.reshape(rows * width, chans)
    normed = layer_norm(flat.astype(jnp.float32), norm_gain, norm_bias, 1).astype(jnp.bfloat16)
    w_in = jnp.concatenate([left_proj, left_gate, right_proj, right_gate], axis=1)
    projected = jnp.einsum("pc,cf->fp", normed, w_in, preferred_element_type=jnp.float32)
    weight = (row_valid[:, None] * col_valid[None, :]).reshape(1, rows * width)
    left_t = (
        (weight * jax.nn.sigmoid(projected[hidden : 2 * hidden]) * projected[:hidden])
        .astype(jnp.bfloat16)
        .reshape(hidden, rows, width)
    )
    right_t = (
        (weight * jax.nn.sigmoid(projected[3 * hidden :]) * projected[2 * hidden : 3 * hidden])
        .astype(jnp.bfloat16)
        .reshape(hidden, rows, width)
    )
    left_c, right_c = (
        lax.all_to_all(left_t, ("chan", "sub"), split_axis=0, concat_axis=2, tiled=True),
        lax.all_to_all(right_t, ("chan", "sub"), split_axis=0, concat_axis=2, tiled=True),
    )
    tri = jnp.einsum(
        "cik,cjk->cij",
        left_c,
        lax.all_gather(right_c, "row", axis=1, tiled=True),
        preferred_element_type=jnp.float32,
    ).astype(jnp.bfloat16)
    back = lax.all_to_all(tri, ("chan", "sub"), split_axis=2, concat_axis=0, tiled=True)
    tri_flat = back.reshape(hidden, rows * width)
    result = finish(flat, normed, tri_flat, out_norm_gain, out_norm_bias, out_proj, out_gate)
    relaid = lax.all_to_all(
        result.reshape(rows, width, chans), "row", split_axis=1, concat_axis=0, tiled=True
    )
    return relaid


MESH = pl.DeviceIdType.MESH


def place(rows, chans, subs):
    row, chan, sub = lax.axis_index("row"), lax.axis_index("chan"), lax.axis_index("sub")
    return (row * chans + chan) * subs + sub


def coords(member, chans, subs):
    return {
        "row": member // (chans * subs),
        "chan": (member // subs) % chans,
        "sub": member % subs,
    }


def greet(me, count, chans, subs):
    barrier = pltpu.get_barrier_semaphore()
    for step in range(1, count):
        peer = lax.rem(me + step, count)
        pl.semaphore_signal(
            barrier, inc=1, device_id=coords(peer, chans, subs), device_id_type=MESH
        )
    pl.semaphore_wait(barrier, count - 1)


def norm_rows(values, gain, bias):
    mean = jnp.mean(values, axis=1, keepdims=True)
    centred = values - mean
    spread = jnp.mean(centred * centred, axis=1, keepdims=True)
    return centred * lax.rsqrt(spread + EPS) * gain + bias


def residues_held(positions, chain_len, slot):
    held = jnp.zeros(positions.shape, jnp.float32)
    for chain in range(chain_len.shape[0]):
        first = chain * slot
        inside = (positions >= first) & (positions < first + chain_len[chain])
        held = jnp.where(inside, 1.0, held)
    return held


def update_kernel(
    dims,
    chain_len,
    pair,
    params,
    weights,
    result,
    out,
    sides,
    moved,
    w_t,
    picks,
    spread,
    tri_rows,
    tri_out,
    tri_got,
    gates,
    side_sems,
    pair_sems,
    tri_sems,
    own_sems,
):
    rows, chans, subs = dims
    blocks = chans * subs
    count = rows * blocks
    me = place(rows, chans, subs)
    my_row = me // blocks
    my_block = lax.rem(me, blocks)
    greet(me, count, chans, subs)
    width, height, depth = pair.shape
    share = width // rows
    slot = rows * height // chain_len.shape[0]
    steps, lanes = out.shape[1], out.shape[3]
    columns = lanes // height
    hidden = weights.shape[2]
    per = hidden // count
    total = rows * height
    sends = []

    def remote(source, target, sems, device):
        copy = pltpu.make_async_remote_copy(
            src_ref=source,
            dst_ref=target,
            send_sem=sems[0],
            recv_sem=sems[1],
            device_id=device,
            device_id_type=MESH,
        )
        copy.start()
        sends.append(copy)
        return copy

    pair_waits = []
    my_span = pl.ds(pl.multiple_of(my_row * height, height), height)

    def send_pair(part):
        size = share // 2
        for step in range(1, rows):
            target = lax.rem(my_row + step, rows)
            pair_waits.append(
                remote(
                    pair.at[pl.ds(target * share + part * size, size)],
                    moved.at[pl.ds(part * size, size), my_span],
                    (pair_sems.at[0, part, step], pair_sems.at[1, part, step]),
                    {"row": target},
                )
            )

    own_pair = pltpu.make_async_copy(
        pair.at[pl.ds(my_row * share, share)], moved.at[:, my_span], own_sems.at[0]
    )
    own_pair.start()
    send_pair(0)
    for index in range(4):
        w_t[pl.ds(index * hidden, hidden)] = (
            weights[index].astype(jnp.float32).T.astype(jnp.bfloat16)
        )
    gain, bias = params[0:1], params[1:2]
    out_gain, out_bias = params[2:3], params[3:4]
    lane = lax.broadcasted_iota(jnp.int32, (1, lanes), 1)
    column = jnp.zeros((1, lanes), jnp.int32)
    for edge in range(1, columns):
        column = column + (lane >= edge * height).astype(jnp.int32)
    row_held = residues_held(lane - column * height + my_row * height, chain_len, slot)

    def side_body(index, carry):
        block = pair[pl.ds(index * columns, columns)]
        flat = block.astype(jnp.float32).reshape(lanes, depth)
        normed = norm_rows(flat, gain, bias).astype(jnp.bfloat16)
        projected = lax.dot_general(
            w_t[...], normed, (((1,), (1,)), ((), ())), preferred_element_type=jnp.float32
        )
        held = residues_held(column + (my_block * width + index * columns), chain_len, slot)
        valid = held * row_held
        left = valid * jax.nn.sigmoid(projected[hidden : 2 * hidden]) * projected[:hidden]
        right = (
            valid * jax.nn.sigmoid(projected[3 * hidden :]) * projected[2 * hidden : 3 * hidden]
        )
        both = jnp.concatenate(
            [left.reshape(count, per, lanes), right.reshape(count, per, lanes)], axis=1
        )
        out[:, index] = both.astype(jnp.bfloat16)
        return carry

    side_waits = []
    my_lanes = pl.ds(pl.multiple_of(my_row * lanes, 128), lanes)
    size = steps // 2
    for piece in range(2):
        lax.fori_loop(piece * size, (piece + 1) * size, side_body, 0)
        span = pl.ds(piece * size, size)
        for step in range(1, count):
            peer = lax.rem(me + step, count)
            side_waits.append(
                remote(
                    out.at[peer, span],
                    sides.at[my_block, span, :, my_lanes],
                    (side_sems.at[0, piece, step], side_sems.at[1, piece, step]),
                    coords(peer, chans, subs),
                )
            )
    own_side = pltpu.make_async_copy(
        out.at[me], sides.at[my_block, :, :, my_lanes], own_sems.at[1]
    )
    own_side.start()
    send_pair(1)

    packed = lax.broadcasted_iota(jnp.int32, (lanes, 2 * 128), 0)
    place_of = lax.broadcasted_iota(jnp.int32, (lanes, 2 * 128), 1)

    def pick_body(index, carry):
        at, row = index // rows, index % rows
        low = row * height
        hit = (packed - place_of == at * height - low) & (place_of >= low)
        hit = hit & (place_of < low + height)
        spot = pl.ds(pl.multiple_of(row * lanes, 128), lanes)
        picks[at, spot] = jnp.where(hit, 1.0, 0.0).astype(jnp.bfloat16)
        return carry

    lax.fori_loop(0, columns * rows, pick_body, 0)
    for copy in side_waits:
        copy.wait_recv()
    own_side.wait()

    found = blocks * steps * 2 * per

    def spread_body(index, carry):
        held = jnp.dot(
            sides[...].reshape(found, rows * lanes), picks[index], preferred_element_type=jnp.float32
        )
        spot = pl.ds(pl.multiple_of(index * found, 8), found)
        spread[0, spot] = held[:, :128]
        spread[1, spot] = held[:, 128:]
        return carry

    lax.fori_loop(0, columns, spread_body, 0)
    depth_k = blocks * width

    for channel in range(per):
        def side(first):
            spot = pl.ds(first, depth_k, stride=2 * per)
            return jnp.concatenate([spread[0, spot, :], spread[1, spot, :]], axis=1).astype(
                jnp.bfloat16
            )

        tri = lax.dot_general(
            side(per + channel),
            side(channel),
            (((0,), (0,)), ((), ())),
            preferred_element_type=jnp.float32,
        )
        spot = pl.ds(channel, total, stride=per)
        tri_rows[0, spot, :] = tri[:total, :128]
        tri_rows[1, spot, :] = tri[:total, 128:]

    narrow = lax.broadcasted_iota(jnp.int32, (per, 128), 1) < 64
    tri_waits = []
    own_tri = []
    for unit in range(share // 4):

        def pack_body(index, carry):
            halves = []
            for half in range(2):
                first = index * share + half * (share // 2) + 2 * unit
                one = pl.ds(pl.multiple_of(first * per, per), per)
                two = pl.ds(pl.multiple_of((first + 1) * per, per), per)
                rest = jnp.where(narrow, tri_rows[1, one], pltpu.roll(tri_rows[1, two], 64, 1))
                halves.append(jnp.concatenate([tri_rows[0, one], tri_rows[0, two], rest], axis=1))
            tri_out[index, unit] = jnp.concatenate(halves, axis=0).astype(jnp.bfloat16)
            return carry

        lax.fori_loop(0, count, pack_body, 0)
        arriving = []
        for step in range(1, count):
            peer = lax.rem(me + step, count)
            arriving.append(
                remote(
                    tri_out.at[lax.rem(peer, blocks) * rows + peer // blocks, unit],
                    tri_got.at[me, unit],
                    (tri_sems.at[0, unit, step], tri_sems.at[1, unit, step]),
                    coords(peer, chans, subs),
                )
            )
        tri_waits.append(arriving)
        own = pltpu.make_async_copy(
            tri_out.at[my_block * rows + my_row, unit], tri_got.at[me, unit], own_sems.at[2 + unit]
        )
        own.start()
        own_tri.append(own)

    for copy in pair_waits:
        copy.wait_recv()
    own_pair.wait()

    def base_of(half, unit):
        first = half * (share // 2) + 2 * unit
        return jnp.concatenate(
            [
                moved[first, :128],
                moved[first + 1, :128],
                moved[first, 128:],
                moved[first + 1, 128:],
            ],
            axis=0,
        ).astype(jnp.float32)

    for unit in range(share // 4):
        for half in range(2):
            normed = norm_rows(base_of(half, unit), gain, bias).astype(jnp.bfloat16)
            gates[unit, half] = jax.nn.sigmoid(
                jnp.dot(normed, weights[5], preferred_element_type=jnp.float32)
            )
    for unit in range(share // 4):
        for copy in tri_waits[unit]:
            copy.wait_recv()
        own_tri[unit].wait()
        tri = tri_got[:, unit].astype(jnp.float32)
        for half in range(2):
            piece = tri[:, half * per : (half + 1) * per].reshape(hidden, 2 * total)
            mean = jnp.mean(piece, axis=0, keepdims=True)
            centred = piece - mean
            square = jnp.mean(centred * centred, axis=0, keepdims=True)
            scaled = (centred * lax.rsqrt(square + EPS)).T
            tri_normed = (scaled * out_gain + out_bias).astype(jnp.bfloat16)
            update = jnp.dot(tri_normed, weights[4], preferred_element_type=jnp.float32)
            done = (base_of(half, unit) + gates[unit, half] * update).astype(jnp.bfloat16)
            first = half * (share // 2) + 2 * unit
            result[first, :128] = done[:128]
            result[first + 1, :128] = done[128:256]
            result[first, 128:] = done[256 : 128 + total]
            result[first + 1, 128:] = done[128 + total :]
    for copy in sends:
        copy.wait_send()


def shards_direct(pair, chain_len, *params):
    height, width, depth = pair.shape
    norm_gain, norm_bias, left_proj, left_gate, right_proj, right_gate = params[:6]
    out_norm_gain, out_norm_bias, out_proj, out_gate = params[6:]
    hidden = left_proj.shape[1]
    dims = (lax.axis_size("row"), lax.axis_size("chan"), lax.axis_size("sub"))
    blocks = dims[1] * dims[2]
    count = dims[0] * blocks
    per = hidden // count
    total = height * dims[0]
    share = width // dims[0]
    columns = 8
    lanes = columns * height
    steps = width // columns
    units = share // 4
    vectors = jnp.stack([norm_gain, norm_bias, out_norm_gain, out_norm_bias])
    weights = jnp.stack([left_proj, left_gate, right_proj, right_gate, out_proj, out_gate])
    whole = pl.BlockSpec(memory_space=pltpu.VMEM)
    result = pl.pallas_call(
        functools.partial(update_kernel, dims),
        out_shape=jax.ShapeDtypeStruct((share, total, depth), jnp.bfloat16),
        in_specs=[pl.BlockSpec(memory_space=pltpu.SMEM)] + [whole] * 3,
        out_specs=whole,
        scratch_shapes=[
            pltpu.VMEM((count, steps, 2 * per, lanes), jnp.bfloat16),
            pltpu.VMEM((blocks, steps, 2 * per, dims[0] * lanes), jnp.bfloat16),
            pltpu.VMEM((share, total, depth), jnp.bfloat16),
            pltpu.VMEM((4 * hidden, depth), jnp.bfloat16),
            pltpu.VMEM((columns, dims[0] * lanes, 256), jnp.bfloat16),
            pltpu.VMEM((2, blocks * width * 2 * per, 128), jnp.float32),
            pltpu.VMEM((2, total * per, 128), jnp.float32),
            pltpu.VMEM((count, units, 2 * per, 2 * total), jnp.bfloat16),
            pltpu.VMEM((count, units, 2 * per, 2 * total), jnp.bfloat16),
            pltpu.VMEM((units, 2, 2 * total, depth), jnp.float32),
            pltpu.SemaphoreType.DMA((2, 2, count)),
            pltpu.SemaphoreType.DMA((2, 2, dims[0])),
            pltpu.SemaphoreType.DMA((2, units, count)),
            pltpu.SemaphoreType.DMA((2 + units,)),
        ],
        compiler_params=pltpu.CompilerParams(
            collective_id=0, has_side_effects=True, vmem_limit_bytes=48 << 20
        ),
        name="update",
    )(chain_len, pair.transpose(1, 0, 2), vectors, weights)
    return result.transpose(1, 0, 2)


def shards(pair, chain_len, *params):
    height, width, _ = pair.shape
    hidden = params[2].shape[1]
    rows = lax.axis_size("row")
    count = rows * lax.axis_size("chan") * lax.axis_size("sub")
    fits = (
        count * 8 == hidden
        and height % 16 == 0
        and (8 * height) % 128 == 0
        and width % 16 == 0
        and width % (4 * rows) == 0
        and height * rows == 192
        and width * count == 192 * rows
    )
    body = shards_direct if fits else shards_general
    return body(pair, chain_len, *params)


def solution(mesh):
    return jax.shard_map(
        shards,
        mesh=mesh,
        in_specs=(
            P(("groups", "row"), ("chan", "sub"), None),
            P("groups"),
            P(),
            P(),
            P(),
            P(),
            P(),
            P(),
            P(),
            P(),
            P(),
            P(),
        ),
        out_specs=P("groups", ("chan", "sub", "row"), None),
        check_vma=False,
    )
```

```python
import functools

import jax
import jax.numpy as jnp
from jax import lax
from jax.experimental import pallas as pl
from jax.experimental.pallas import tpu as pltpu
from jax.sharding import PartitionSpec as P

EPS = 1e-05


def layer_norm(values, gain, bias, axis):
    mean = jnp.mean(values, axis=axis, keepdims=True)
    centred = values - mean
    spread = jnp.mean(centred * centred, axis=axis, keepdims=True)
    return centred * lax.rsqrt(spread + EPS) * gain + bias


def residue_valid(positions, chain_len, slot):
    owner = positions // slot
    picks = owner[:, None] == jnp.arange(chain_len.shape[0], dtype=jnp.int32)[None, :]
    limit = jnp.sum(jnp.where(picks, chain_len[None, :], 0), axis=1)
    return (positions % slot < limit).astype(jnp.float32)


def finish(base_flat, base_normed, tri_flat, out_norm_gain, out_norm_bias, out_proj, out_gate):
    gate = jax.nn.sigmoid(jnp.dot(base_normed, out_gate, preferred_element_type=jnp.float32))
    tri_normed = layer_norm(
        tri_flat.astype(jnp.float32), out_norm_gain[:, None], out_norm_bias[:, None], 0
    ).astype(jnp.bfloat16)
    update = jnp.einsum("hp,hc->pc", tri_normed, out_proj, preferred_element_type=jnp.float32)
    return (base_flat.astype(jnp.float32) + gate * update).astype(jnp.bfloat16)


def shards_general(
    pair,
    chain_len,
    norm_gain,
    norm_bias,
    left_proj,
    left_gate,
    right_proj,
    right_gate,
    out_norm_gain,
    out_norm_bias,
    out_proj,
    out_gate,
):
    rows, width, chans = pair.shape
    hidden = left_proj.shape[1]
    row_count = lax.axis_size("row")
    total = rows * row_count
    slot = total // chain_len.shape[0]
    column_block = lax.axis_index("chan") * lax.axis_size("sub") + lax.axis_index("sub")
    row_ids = lax.axis_index("row") * rows + jnp.arange(rows, dtype=jnp.int32)
    col_ids = column_block * width + jnp.arange(width, dtype=jnp.int32)
    row_valid = residue_valid(row_ids, chain_len, slot)
    col_valid = residue_valid(col_ids, chain_len, slot)
    flat = pair.reshape(rows * width, chans)
    normed = layer_norm(flat.astype(jnp.float32), norm_gain, norm_bias, 1).astype(jnp.bfloat16)
    w_in = jnp.concatenate([left_proj, left_gate, right_proj, right_gate], axis=1)
    projected = jnp.einsum("pc,cf->fp", normed, w_in, preferred_element_type=jnp.float32)
    weight = (row_valid[:, None] * col_valid[None, :]).reshape(1, rows * width)
    left_t = (
        (weight * jax.nn.sigmoid(projected[hidden : 2 * hidden]) * projected[:hidden])
        .astype(jnp.bfloat16)
        .reshape(hidden, rows, width)
    )
    right_t = (
        (weight * jax.nn.sigmoid(projected[3 * hidden :]) * projected[2 * hidden : 3 * hidden])
        .astype(jnp.bfloat16)
        .reshape(hidden, rows, width)
    )
    left_c, right_c = (
        lax.all_to_all(left_t, ("chan", "sub"), split_axis=0, concat_axis=2, tiled=True),
        lax.all_to_all(right_t, ("chan", "sub"), split_axis=0, concat_axis=2, tiled=True),
    )
    tri = jnp.einsum(
        "cik,cjk->cij",
        left_c,
        lax.all_gather(right_c, "row", axis=1, tiled=True),
        preferred_element_type=jnp.float32,
    ).astype(jnp.bfloat16)
    back = lax.all_to_all(tri, ("chan", "sub"), split_axis=2, concat_axis=0, tiled=True)
    tri_flat = back.reshape(hidden, rows * width)
    result = finish(flat, normed, tri_flat, out_norm_gain, out_norm_bias, out_proj, out_gate)
    relaid = lax.all_to_all(
        result.reshape(rows, width, chans), "row", split_axis=1, concat_axis=0, tiled=True
    )
    return relaid


MESH = pl.DeviceIdType.MESH


def place(rows, chans, subs):
    row, chan, sub = lax.axis_index("row"), lax.axis_index("chan"), lax.axis_index("sub")
    return (row * chans + chan) * subs + sub


def coords(member, chans, subs):
    return {
        "row": member // (chans * subs),
        "chan": (member // subs) % chans,
        "sub": member % subs,
    }


def greet(me, count, chans, subs):
    barrier = pltpu.get_barrier_semaphore()
    for step in range(1, count):
        peer = lax.rem(me + step, count)
        pl.semaphore_signal(
            barrier, inc=1, device_id=coords(peer, chans, subs), device_id_type=MESH
        )
    pl.semaphore_wait(barrier, count - 1)


def norm_rows(values, gain, bias):
    mean = jnp.mean(values, axis=1, keepdims=True)
    centred = values - mean
    spread = jnp.mean(centred * centred, axis=1, keepdims=True)
    return centred * lax.rsqrt(spread + EPS) * gain + bias


def residues_held(positions, chain_len, slot):
    held = jnp.zeros(positions.shape, jnp.float32)
    for chain in range(chain_len.shape[0]):
        first = chain * slot
        inside = (positions >= first) & (positions < first + chain_len[chain])
        held = jnp.where(inside, 1.0, held)
    return held


def update_kernel(
    dims,
    chain_len,
    pair,
    *refs,
):
    held_far, refs = refs[:10], refs[10:]
    update_body(dims, chain_len, pair, held_far, *refs)


def update_body(
    dims,
    chain_len,
    pair,
    held_far,
    result,
    params,
    weights,
    out,
    sides,
    moved,
    w_t,
    picks,
    spread,
    tri_rows,
    tri_out,
    tri_got,
    gates,
    side_sems,
    pair_sems,
    tri_sems,
    own_sems,
    own_sides,
    load_sems,
):
    rows, chans, subs = dims
    blocks = chans * subs
    count = rows * blocks
    me = place(rows, chans, subs)
    loads = []
    for index, source in enumerate(held_far):
        target = params.at[index] if index < 4 else weights.at[index - 4]
        loads.append(pltpu.make_async_copy(source, target, load_sems.at[index]))
        loads[-1].start()
    my_row = me // blocks
    my_block = lax.rem(me, blocks)
    greet(me, count, chans, subs)
    width, height, depth = pair.shape
    share = width // rows
    slot = rows * height // chain_len.shape[0]
    steps, lanes = out.shape[1], out.shape[3]
    columns = lanes // height
    hidden = weights.shape[2]
    per = hidden // count
    total = rows * height
    sends = []
    offsets = [rows // 2] + [step for step in range(rows - 1, 0, -1) if step != rows // 2] + [0]
    peers = []
    for row_step in offsets:
        for block_step in range(blocks):
            if row_step or block_step:
                row = lax.rem(my_row + row_step, rows)
                peers.append((row, lax.rem(my_block + block_step, blocks)))

    def remote(source, target, sems, device):
        copy = pltpu.make_async_remote_copy(
            src_ref=source,
            dst_ref=target,
            send_sem=sems[0],
            recv_sem=sems[1],
            device_id=device,
            device_id_type=MESH,
        )
        copy.start()
        sends.append(copy)
        return copy

    pair_waits = []
    my_span = pl.ds(pl.multiple_of(my_row * height, height), height)

    def send_pair(part):
        size = share // 2
        for step in offsets[:-1]:
            target = lax.rem(my_row + step, rows)
            pair_waits.append(
                remote(
                    pair.at[pl.ds(target * share + part * size, size)],
                    moved.at[pl.ds(part * size, size), my_span],
                    (pair_sems.at[0, part, step], pair_sems.at[1, part, step]),
                    {"row": target},
                )
            )

    own_pair = pltpu.make_async_copy(
        pair.at[pl.ds(my_row * share, share)], moved.at[:, my_span], own_sems.at[0]
    )
    own_pair.start()
    send_pair(0)
    for load in loads:
        load.wait()
    for index in range(4):
        w_t[pl.ds(index * hidden, hidden)] = (
            weights[index].astype(jnp.float32).T.astype(jnp.bfloat16)
        )
    gain, bias, out_gain, out_bias = (params[index] for index in range(4))
    lane = lax.broadcasted_iota(jnp.int32, (1, lanes), 1)
    column = jnp.zeros((1, lanes), jnp.int32)
    for edge in range(1, columns):
        column = column + (lane >= edge * height).astype(jnp.int32)
    row_held = residues_held(lane - column * height + my_row * height, chain_len, slot)

    def side_body(index, carry):
        block = pair[pl.ds(index * columns, columns)]
        flat = block.astype(jnp.float32).reshape(lanes, depth)
        normed = norm_rows(flat, gain, bias).astype(jnp.bfloat16)
        projected = lax.dot_general(
            w_t[...], normed, (((1,), (1,)), ((), ())), preferred_element_type=jnp.float32
        )
        held = residues_held(column + (my_block * width + index * columns), chain_len, slot)
        valid = held * row_held
        left = valid * jax.nn.sigmoid(projected[hidden : 2 * hidden]) * projected[:hidden]
        right = (
            valid * jax.nn.sigmoid(projected[3 * hidden :]) * projected[2 * hidden : 3 * hidden]
        )
        both = jnp.concatenate(
            [left.reshape(count, per, lanes), right.reshape(count, per, lanes)], axis=1
        )
        out[:, index] = both.astype(jnp.bfloat16)
        return carry

    side_waits, own_side = [], []
    my_lanes = pl.ds(pl.multiple_of(my_row * lanes, 128), lanes)
    size = steps // 2
    for piece in range(2):
        lax.fori_loop(piece * size, (piece + 1) * size, side_body, 0)
        span = pl.ds(piece * size, size)
        arriving = []
        for step, (row, block) in enumerate(peers):
            arriving.append(
                remote(
                    out.at[row * blocks + block, span],
                    sides.at[piece, my_block, :, :, my_lanes],
                    (side_sems.at[0, piece, step], side_sems.at[1, piece, step]),
                    coords(row * blocks + block, chans, subs),
                )
            )
        side_waits.append(arriving)
        own = pltpu.make_async_copy(
            out.at[me, span], sides.at[piece, my_block, :, :, my_lanes], own_sides.at[piece]
        )
        own.start()
        own_side.append(own)
    send_pair(1)

    packed = lax.broadcasted_iota(jnp.int32, (lanes, 2 * 128), 0)
    place_of = lax.broadcasted_iota(jnp.int32, (lanes, 2 * 128), 1)

    def pick_body(index, carry):
        at, row = index // rows, index % rows
        low = row * height
        hit = (packed - place_of == at * height - low) & (place_of >= low)
        hit = hit & (place_of < low + height)
        spot = pl.ds(pl.multiple_of(row * lanes, 128), lanes)
        picks[at, spot] = jnp.where(hit, 1.0, 0.0).astype(jnp.bfloat16)
        return carry

    lax.fori_loop(0, columns * rows, pick_body, 0)
    found = blocks * size * 2 * per
    for piece in range(2):
        for copy in side_waits[piece]:
            copy.wait_recv()
        own_side[piece].wait()

        def spread_body(index, carry):
            held = jnp.dot(
                sides[piece].reshape(found, rows * lanes),
                picks[index],
                preferred_element_type=jnp.float32,
            )
            spot = pl.ds(pl.multiple_of((piece * columns + index) * found, 8), found)
            spread[0, spot] = held[:, :128]
            spread[1, spot] = held[:, 128:]
            return carry

        lax.fori_loop(0, columns, spread_body, 0)
    depth_k = blocks * width

    for channel in range(per):
        def side(first):
            spot = pl.ds(first, depth_k, stride=2 * per)
            return jnp.concatenate([spread[0, spot, :], spread[1, spot, :]], axis=1).astype(
                jnp.bfloat16
            )

        tri = lax.dot_general(
            side(per + channel),
            side(channel),
            (((0,), (0,)), ((), ())),
            preferred_element_type=jnp.float32,
        )
        spot = pl.ds(channel, total, stride=per)
        tri_rows[0, spot, :] = tri[:total, :128]
        tri_rows[1, spot, :] = tri[:total, 128:]

    narrow = lax.broadcasted_iota(jnp.int32, (per, 128), 1) < 64
    tri_waits = []
    own_tri = []
    for unit in range(share // 4):

        def pack_body(index, carry):
            halves = []
            for half in range(2):
                first = index * share + half * (share // 2) + 2 * unit
                one = pl.ds(pl.multiple_of(first * per, per), per)
                two = pl.ds(pl.multiple_of((first + 1) * per, per), per)
                rest = jnp.where(narrow, tri_rows[1, one], pltpu.roll(tri_rows[1, two], 64, 1))
                halves.append(jnp.concatenate([tri_rows[0, one], tri_rows[0, two], rest], axis=1))
            tri_out[index, unit] = jnp.concatenate(halves, axis=0).astype(jnp.bfloat16)
            return carry

        lax.fori_loop(0, count, pack_body, 0)
        arriving = []
        for step, (row, block) in enumerate(peers):
            arriving.append(
                remote(
                    tri_out.at[block * rows + row, unit],
                    tri_got.at[me, unit],
                    (tri_sems.at[0, unit, step], tri_sems.at[1, unit, step]),
                    coords(row * blocks + block, chans, subs),
                )
            )
        tri_waits.append(arriving)
        own = pltpu.make_async_copy(
            tri_out.at[my_block * rows + my_row, unit], tri_got.at[me, unit], own_sems.at[2 + unit]
        )
        own.start()
        own_tri.append(own)

    for copy in pair_waits:
        copy.wait_recv()
    own_pair.wait()

    def base_of(half, unit):
        first = half * (share // 2) + 2 * unit
        return jnp.concatenate(
            [
                moved[first, :128],
                moved[first + 1, :128],
                moved[first, 128:],
                moved[first + 1, 128:],
            ],
            axis=0,
        ).astype(jnp.float32)

    for unit in range(share // 4):
        for half in range(2):
            normed = norm_rows(base_of(half, unit), gain, bias).astype(jnp.bfloat16)
            gates[unit, half] = jax.nn.sigmoid(
                jnp.dot(normed, weights[5], preferred_element_type=jnp.float32)
            )
    for unit in range(share // 4):
        for copy in tri_waits[unit]:
            copy.wait_recv()
        own_tri[unit].wait()
        tri = tri_got[:, unit].astype(jnp.float32)
        for half in range(2):
            piece = tri[:, half * per : (half + 1) * per].reshape(hidden, 2 * total)
            mean = jnp.mean(piece, axis=0, keepdims=True)
            centred = piece - mean
            square = jnp.mean(centred * centred, axis=0, keepdims=True)
            scaled = (centred * lax.rsqrt(square + EPS)).T
            tri_normed = (scaled * out_gain + out_bias).astype(jnp.bfloat16)
            update = jnp.dot(tri_normed, weights[4], preferred_element_type=jnp.float32)
            done = (base_of(half, unit) + gates[unit, half] * update).astype(jnp.bfloat16)
            first = half * (share // 2) + 2 * unit
            result[first, :128] = done[:128]
            result[first + 1, :128] = done[128:256]
            result[first, 128:] = done[256 : 128 + total]
            result[first + 1, 128:] = done[128 + total :]
    for copy in sends:
        copy.wait_send()


def shards_direct(pair, chain_len, *params):
    height, width, depth = pair.shape
    hidden = params[2].shape[1]
    dims = (lax.axis_size("row"), lax.axis_size("chan"), lax.axis_size("sub"))
    blocks = dims[1] * dims[2]
    count = dims[0] * blocks
    per = hidden // count
    total = height * dims[0]
    share = width // dims[0]
    columns = 8
    lanes = columns * height
    steps = width // columns
    units = share // 4
    vectors = [vector[None, :] for vector in params[:2] + params[6:8]]
    weights = params[2:6] + params[8:]
    far = pl.BlockSpec(memory_space=pl.ANY)
    whole = pl.BlockSpec(memory_space=pltpu.VMEM)
    result = pl.pallas_call(
        functools.partial(update_kernel, dims),
        out_shape=jax.ShapeDtypeStruct((share, total, depth), jnp.bfloat16),
        in_specs=[pl.BlockSpec(memory_space=pltpu.SMEM)] + [whole] + [far] * 10,
        out_specs=whole,
        scratch_shapes=[
            pltpu.VMEM((4, 1, depth), jnp.float32),
            pltpu.VMEM((6, depth, hidden), jnp.bfloat16),
            pltpu.VMEM((count, steps, 2 * per, lanes), jnp.bfloat16),
            pltpu.VMEM((2, blocks, steps // 2, 2 * per, dims[0] * lanes), jnp.bfloat16),
            pltpu.VMEM((share, total, depth), jnp.bfloat16),
            pltpu.VMEM((4 * hidden, depth), jnp.bfloat16),
            pltpu.VMEM((columns, dims[0] * lanes, 256), jnp.bfloat16),
            pltpu.VMEM((2, blocks * width * 2 * per, 128), jnp.float32),
            pltpu.VMEM((2, total * per, 128), jnp.float32),
            pltpu.VMEM((count, units, 2 * per, 2 * total), jnp.bfloat16),
            pltpu.VMEM((count, units, 2 * per, 2 * total), jnp.bfloat16),
            pltpu.VMEM((units, 2, 2 * total, depth), jnp.float32),
            pltpu.SemaphoreType.DMA((2, 2, count)),
            pltpu.SemaphoreType.DMA((2, 2, dims[0])),
            pltpu.SemaphoreType.DMA((2, units, count)),
            pltpu.SemaphoreType.DMA((2 + units,)),
            pltpu.SemaphoreType.DMA((2,)),
            pltpu.SemaphoreType.DMA((10,)),
        ],
        compiler_params=pltpu.CompilerParams(
            collective_id=0, has_side_effects=True, vmem_limit_bytes=48 << 20
        ),
        name="update",
    )(chain_len, pair.transpose(1, 0, 2), *vectors, *weights)
    return result.transpose(1, 0, 2)


def shards(pair, chain_len, *params):
    height, width, _ = pair.shape
    hidden = params[2].shape[1]
    rows = lax.axis_size("row")
    count = rows * lax.axis_size("chan") * lax.axis_size("sub")
    fits = (
        count * 8 == hidden
        and height % 16 == 0
        and (8 * height) % 128 == 0
        and width % 16 == 0
        and width % (4 * rows) == 0
        and height * rows == 192
        and width * count == 192 * rows
    )
    body = shards_direct if fits else shards_general
    return body(pair, chain_len, *params)


def solution(mesh):
    return jax.shard_map(
        shards,
        mesh=mesh,
        in_specs=(
            P(("groups", "row"), ("chan", "sub"), None),
            P("groups"),
            P(),
            P(),
            P(),
            P(),
            P(),
            P(),
            P(),
            P(),
            P(),
            P(),
        ),
        out_specs=P("groups", ("chan", "sub", "row"), None),
        check_vma=False,
    )
```

```python
import functools

import jax
import jax.numpy as jnp
from jax import lax
from jax.experimental import pallas as pl
from jax.experimental.pallas import tpu as pltpu
from jax.sharding import PartitionSpec as P

EPS = 1e-05


def layer_norm(values, gain, bias, axis):
    mean = jnp.mean(values, axis=axis, keepdims=True)
    centred = values - mean
    spread = jnp.mean(centred * centred, axis=axis, keepdims=True)
    return centred * lax.rsqrt(spread + EPS) * gain + bias


def residue_valid(positions, chain_len, slot):
    owner = positions // slot
    picks = owner[:, None] == jnp.arange(chain_len.shape[0], dtype=jnp.int32)[None, :]
    limit = jnp.sum(jnp.where(picks, chain_len[None, :], 0), axis=1)
    return (positions % slot < limit).astype(jnp.float32)


def finish(base_flat, base_normed, tri_flat, out_norm_gain, out_norm_bias, out_proj, out_gate):
    gate = jax.nn.sigmoid(jnp.dot(base_normed, out_gate, preferred_element_type=jnp.float32))
    tri_normed = layer_norm(
        tri_flat.astype(jnp.float32), out_norm_gain[:, None], out_norm_bias[:, None], 0
    ).astype(jnp.bfloat16)
    update = jnp.einsum("hp,hc->pc", tri_normed, out_proj, preferred_element_type=jnp.float32)
    return (base_flat.astype(jnp.float32) + gate * update).astype(jnp.bfloat16)


def shards_general(
    pair,
    chain_len,
    norm_gain,
    norm_bias,
    left_proj,
    left_gate,
    right_proj,
    right_gate,
    out_norm_gain,
    out_norm_bias,
    out_proj,
    out_gate,
):
    rows, width, chans = pair.shape
    hidden = left_proj.shape[1]
    row_count = lax.axis_size("row")
    total = rows * row_count
    slot = total // chain_len.shape[0]
    column_block = lax.axis_index("chan") * lax.axis_size("sub") + lax.axis_index("sub")
    row_ids = lax.axis_index("row") * rows + jnp.arange(rows, dtype=jnp.int32)
    col_ids = column_block * width + jnp.arange(width, dtype=jnp.int32)
    row_valid = residue_valid(row_ids, chain_len, slot)
    col_valid = residue_valid(col_ids, chain_len, slot)
    flat = pair.reshape(rows * width, chans)
    normed = layer_norm(flat.astype(jnp.float32), norm_gain, norm_bias, 1).astype(jnp.bfloat16)
    w_in = jnp.concatenate([left_proj, left_gate, right_proj, right_gate], axis=1)
    projected = jnp.einsum("pc,cf->fp", normed, w_in, preferred_element_type=jnp.float32)
    weight = (row_valid[:, None] * col_valid[None, :]).reshape(1, rows * width)
    left_t = (
        (weight * jax.nn.sigmoid(projected[hidden : 2 * hidden]) * projected[:hidden])
        .astype(jnp.bfloat16)
        .reshape(hidden, rows, width)
    )
    right_t = (
        (weight * jax.nn.sigmoid(projected[3 * hidden :]) * projected[2 * hidden : 3 * hidden])
        .astype(jnp.bfloat16)
        .reshape(hidden, rows, width)
    )
    left_c, right_c = (
        lax.all_to_all(left_t, ("chan", "sub"), split_axis=0, concat_axis=2, tiled=True),
        lax.all_to_all(right_t, ("chan", "sub"), split_axis=0, concat_axis=2, tiled=True),
    )
    tri = jnp.einsum(
        "cik,cjk->cij",
        left_c,
        lax.all_gather(right_c, "row", axis=1, tiled=True),
        preferred_element_type=jnp.float32,
    ).astype(jnp.bfloat16)
    back = lax.all_to_all(tri, ("chan", "sub"), split_axis=2, concat_axis=0, tiled=True)
    tri_flat = back.reshape(hidden, rows * width)
    result = finish(flat, normed, tri_flat, out_norm_gain, out_norm_bias, out_proj, out_gate)
    relaid = lax.all_to_all(
        result.reshape(rows, width, chans), "row", split_axis=1, concat_axis=0, tiled=True
    )
    return relaid


MESH = pl.DeviceIdType.MESH


def place(rows, chans, subs):
    row, chan, sub = lax.axis_index("row"), lax.axis_index("chan"), lax.axis_index("sub")
    return (row * chans + chan) * subs + sub


def coords(member, chans, subs):
    return {
        "row": member // (chans * subs),
        "chan": (member // subs) % chans,
        "sub": member % subs,
    }


def greet(me, count, chans, subs):
    barrier = pltpu.get_barrier_semaphore()
    for step in range(1, count):
        peer = lax.rem(me + step, count)
        pl.semaphore_signal(
            barrier, inc=1, device_id=coords(peer, chans, subs), device_id_type=MESH
        )
    return barrier


def norm_rows(values, gain, bias):
    mean = jnp.mean(values, axis=1, keepdims=True)
    centred = values - mean
    spread = jnp.mean(centred * centred, axis=1, keepdims=True)
    return centred * lax.rsqrt(spread + EPS) * gain + bias


def residues_held(positions, chain_len, slot):
    held = jnp.zeros(positions.shape, jnp.float32)
    for chain in range(chain_len.shape[0]):
        first = chain * slot
        inside = (positions >= first) & (positions < first + chain_len[chain])
        held = jnp.where(inside, 1.0, held)
    return held


def update_kernel(
    dims,
    chain_len,
    pair,
    *refs,
):
    held_far, refs = refs[:10], refs[10:]
    update_body(dims, chain_len, pair, held_far, *refs)


def update_body(
    dims,
    chain_len,
    pair,
    held_far,
    result,
    params,
    weights,
    out,
    sides,
    moved,
    w_t,
    picks,
    spread,
    tri_rows,
    tri_out,
    tri_got,
    gates,
    side_sems,
    pair_sems,
    tri_sems,
    own_sems,
    own_sides,
    load_sems,
):
    rows, chans, subs = dims
    blocks = chans * subs
    count = rows * blocks
    me = place(rows, chans, subs)
    loads = []
    for index, source in enumerate(held_far):
        target = params.at[index] if index < 4 else weights.at[index - 4]
        loads.append(pltpu.make_async_copy(source, target, load_sems.at[index]))
        loads[-1].start()
    my_row = me // blocks
    my_block = lax.rem(me, blocks)
    barrier = greet(me, count, chans, subs)
    width, height, depth = pair.shape
    share = width // rows
    slot = rows * height // chain_len.shape[0]
    steps, lanes = out.shape[1], out.shape[3]
    columns = lanes // height
    hidden = weights.shape[2]
    per = hidden // count
    total = rows * height
    sends = []
    offsets = [rows // 2] + [step for step in range(rows - 1, 0, -1) if step != rows // 2] + [0]
    peers = []
    for row_step in offsets:
        for block_step in range(blocks):
            if row_step or block_step:
                row = lax.rem(my_row + row_step, rows)
                peers.append((row, lax.rem(my_block + block_step, blocks)))

    def remote(source, target, sems, device):
        copy = pltpu.make_async_remote_copy(
            src_ref=source,
            dst_ref=target,
            send_sem=sems[0],
            recv_sem=sems[1],
            device_id=device,
            device_id_type=MESH,
        )
        copy.start()
        sends.append(copy)
        return copy

    pair_waits = []
    my_span = pl.ds(pl.multiple_of(my_row * height, height), height)

    def send_pair(part):
        size = share // 2
        for step in offsets[:-1]:
            target = lax.rem(my_row + step, rows)
            pair_waits.append(
                remote(
                    pair.at[pl.ds(target * share + part * size, size)],
                    moved.at[pl.ds(part * size, size), my_span],
                    (pair_sems.at[0, part, step], pair_sems.at[1, part, step]),
                    {"row": target},
                )
            )

    own_pair = pltpu.make_async_copy(
        pair.at[pl.ds(my_row * share, share)], moved.at[:, my_span], own_sems.at[0]
    )
    own_pair.start()
    for load in loads:
        load.wait()
    for index in range(4):
        w_t[pl.ds(index * hidden, hidden)] = (
            weights[index].astype(jnp.float32).T.astype(jnp.bfloat16)
        )
    gain, bias, out_gain, out_bias = (params[index] for index in range(4))
    lane = lax.broadcasted_iota(jnp.int32, (1, lanes), 1)
    column = jnp.zeros((1, lanes), jnp.int32)
    for edge in range(1, columns):
        column = column + (lane >= edge * height).astype(jnp.int32)
    row_held = residues_held(lane - column * height + my_row * height, chain_len, slot)

    def side_body(index, carry):
        block = pair[pl.ds(index * columns, columns)]
        flat = block.astype(jnp.float32).reshape(lanes, depth)
        normed = norm_rows(flat, gain, bias).astype(jnp.bfloat16)
        projected = lax.dot_general(
            w_t[...], normed, (((1,), (1,)), ((), ())), preferred_element_type=jnp.float32
        )
        held = residues_held(column + (my_block * width + index * columns), chain_len, slot)
        valid = held * row_held
        left = valid * jax.nn.sigmoid(projected[hidden : 2 * hidden]) * projected[:hidden]
        right = (
            valid * jax.nn.sigmoid(projected[3 * hidden :]) * projected[2 * hidden : 3 * hidden]
        )
        both = jnp.concatenate(
            [left.reshape(count, per, lanes), right.reshape(count, per, lanes)], axis=1
        )
        out[:, index] = both.astype(jnp.bfloat16)
        return carry

    side_waits, own_side = [], []
    my_lanes = pl.ds(pl.multiple_of(my_row * lanes, 128), lanes)
    pieces = sides.shape[0]
    size = steps // pieces
    for piece in range(pieces):
        lax.fori_loop(piece * size, (piece + 1) * size, side_body, 0)
        if piece == 0:
            pl.semaphore_wait(barrier, count - 1)
        span = pl.ds(piece * size, size)
        arriving = []
        for step, (row, block) in enumerate(peers):
            arriving.append(
                remote(
                    out.at[row * blocks + block, span],
                    sides.at[piece, my_block, :, :, my_lanes],
                    (side_sems.at[0, piece, step], side_sems.at[1, piece, step]),
                    coords(row * blocks + block, chans, subs),
                )
            )
        side_waits.append(arriving)
        own = pltpu.make_async_copy(
            out.at[me, span], sides.at[piece, my_block, :, :, my_lanes], own_sides.at[piece]
        )
        own.start()
        own_side.append(own)

    send_pair(0)
    packed = lax.broadcasted_iota(jnp.int32, (lanes, 2 * 128), 0)
    place_of = lax.broadcasted_iota(jnp.int32, (lanes, 2 * 128), 1)

    def pick_body(index, carry):
        at, row = index // rows, index % rows
        low = row * height
        hit = (packed - place_of == at * height - low) & (place_of >= low)
        hit = hit & (place_of < low + height)
        spot = pl.ds(pl.multiple_of(row * lanes, 128), lanes)
        picks[at, spot] = jnp.where(hit, 1.0, 0.0).astype(jnp.bfloat16)
        return carry

    lax.fori_loop(0, columns * rows, pick_body, 0)
    found = blocks * size * 2 * per
    for piece in range(pieces):
        for copy in side_waits[piece]:
            copy.wait_recv()
        own_side[piece].wait()
        if piece == pieces - 1:
            send_pair(1)

        def spread_body(index, carry):
            held = jnp.dot(
                sides[piece].reshape(found, rows * lanes),
                picks[index],
                preferred_element_type=jnp.float32,
            )
            spot = pl.ds(pl.multiple_of((piece * columns + index) * found, 8), found)
            spread[0, spot] = held[:, :128]
            spread[1, spot] = held[:, 128:]
            return carry

        lax.fori_loop(0, columns, spread_body, 0)
    depth_k = blocks * width

    for channel in range(per):
        def side(first):
            spot = pl.ds(first, depth_k, stride=2 * per)
            return jnp.concatenate([spread[0, spot, :], spread[1, spot, :]], axis=1).astype(
                jnp.bfloat16
            )

        tri = lax.dot_general(
            side(per + channel),
            side(channel),
            (((0,), (0,)), ((), ())),
            preferred_element_type=jnp.float32,
        )
        spot = pl.ds(channel, total, stride=per)
        tri_rows[0, spot, :] = tri[:total, :128]
        tri_rows[1, spot, :] = tri[:total, 128:]

    narrow = lax.broadcasted_iota(jnp.int32, (per, 128), 1) < 64
    tri_waits = []
    own_tri = []
    for unit in range(share // 4):

        def pack_body(index, carry):
            halves = []
            for half in range(2):
                first = index * share + half * (share // 2) + 2 * unit
                one = pl.ds(pl.multiple_of(first * per, per), per)
                two = pl.ds(pl.multiple_of((first + 1) * per, per), per)
                rest = jnp.where(narrow, tri_rows[1, one], pltpu.roll(tri_rows[1, two], 64, 1))
                halves.append(jnp.concatenate([tri_rows[0, one], tri_rows[0, two], rest], axis=1))
            tri_out[index, unit] = jnp.concatenate(halves, axis=0).astype(jnp.bfloat16)
            return carry

        lax.fori_loop(0, count, pack_body, 0)
        arriving = []
        for step, (row, block) in enumerate(peers):
            arriving.append(
                remote(
                    tri_out.at[block * rows + row, unit],
                    tri_got.at[me, unit],
                    (tri_sems.at[0, unit, step], tri_sems.at[1, unit, step]),
                    coords(row * blocks + block, chans, subs),
                )
            )
        tri_waits.append(arriving)
        own = pltpu.make_async_copy(
            tri_out.at[my_block * rows + my_row, unit], tri_got.at[me, unit], own_sems.at[2 + unit]
        )
        own.start()
        own_tri.append(own)

    for copy in pair_waits:
        copy.wait_recv()
    own_pair.wait()

    def base_of(half, unit):
        first = half * (share // 2) + 2 * unit
        return jnp.concatenate(
            [
                moved[first, :128],
                moved[first + 1, :128],
                moved[first, 128:],
                moved[first + 1, 128:],
            ],
            axis=0,
        ).astype(jnp.float32)

    for unit in range(share // 4):
        for half in range(2):
            normed = norm_rows(base_of(half, unit), gain, bias).astype(jnp.bfloat16)
            gates[unit, half] = jax.nn.sigmoid(
                jnp.dot(normed, weights[5], preferred_element_type=jnp.float32)
            )
    for unit in range(share // 4):
        for copy in tri_waits[unit]:
            copy.wait_recv()
        own_tri[unit].wait()
        tri = tri_got[:, unit].astype(jnp.float32)
        for half in range(2):
            piece = tri[:, half * per : (half + 1) * per].reshape(hidden, 2 * total)
            mean = jnp.mean(piece, axis=0, keepdims=True)
            centred = piece - mean
            square = jnp.mean(centred * centred, axis=0, keepdims=True)
            scaled = (centred * lax.rsqrt(square + EPS)).T
            tri_normed = (scaled * out_gain + out_bias).astype(jnp.bfloat16)
            update = jnp.dot(tri_normed, weights[4], preferred_element_type=jnp.float32)
            done = (base_of(half, unit) + gates[unit, half] * update).astype(jnp.bfloat16)
            first = half * (share // 2) + 2 * unit
            result[first, :128] = done[:128]
            result[first + 1, :128] = done[128:256]
            result[first, 128:] = done[256 : 128 + total]
            result[first + 1, 128:] = done[128 + total :]
    for copy in sends:
        copy.wait_send()


def shards_direct(pair, chain_len, *params):
    height, width, depth = pair.shape
    hidden = params[2].shape[1]
    dims = (lax.axis_size("row"), lax.axis_size("chan"), lax.axis_size("sub"))
    blocks = dims[1] * dims[2]
    count = dims[0] * blocks
    per = hidden // count
    total = height * dims[0]
    share = width // dims[0]
    columns = 8
    lanes = columns * height
    steps = width // columns
    units = share // 4
    pieces = 3
    vectors = [vector[None, :] for vector in params[:2] + params[6:8]]
    weights = params[2:6] + params[8:]
    far = pl.BlockSpec(memory_space=pl.ANY)
    whole = pl.BlockSpec(memory_space=pltpu.VMEM)
    result = pl.pallas_call(
        functools.partial(update_kernel, dims),
        out_shape=jax.ShapeDtypeStruct((share, total, depth), jnp.bfloat16),
        in_specs=[pl.BlockSpec(memory_space=pltpu.SMEM)] + [whole] + [far] * 10,
        out_specs=whole,
        scratch_shapes=[
            pltpu.VMEM((4, 1, depth), jnp.float32),
            pltpu.VMEM((6, depth, hidden), jnp.bfloat16),
            pltpu.VMEM((count, steps, 2 * per, lanes), jnp.bfloat16),
            pltpu.VMEM((pieces, blocks, steps // pieces, 2 * per, dims[0] * lanes), jnp.bfloat16),
            pltpu.VMEM((share, total, depth), jnp.bfloat16),
            pltpu.VMEM((4 * hidden, depth), jnp.bfloat16),
            pltpu.VMEM((columns, dims[0] * lanes, 256), jnp.bfloat16),
            pltpu.VMEM((2, blocks * width * 2 * per, 128), jnp.float32),
            pltpu.VMEM((2, total * per, 128), jnp.float32),
            pltpu.VMEM((count, units, 2 * per, 2 * total), jnp.bfloat16),
            pltpu.VMEM((count, units, 2 * per, 2 * total), jnp.bfloat16),
            pltpu.VMEM((units, 2, 2 * total, depth), jnp.float32),
            pltpu.SemaphoreType.DMA((2, pieces, count)),
            pltpu.SemaphoreType.DMA((2, 2, dims[0])),
            pltpu.SemaphoreType.DMA((2, units, count)),
            pltpu.SemaphoreType.DMA((2 + units,)),
            pltpu.SemaphoreType.DMA((pieces,)),
            pltpu.SemaphoreType.DMA((10,)),
        ],
        compiler_params=pltpu.CompilerParams(
            collective_id=0, has_side_effects=True, vmem_limit_bytes=48 << 20
        ),
        name="update",
    )(chain_len, pair.transpose(1, 0, 2), *vectors, *weights)
    return result.transpose(1, 0, 2)


def shards(pair, chain_len, *params):
    height, width, _ = pair.shape
    hidden = params[2].shape[1]
    rows = lax.axis_size("row")
    count = rows * lax.axis_size("chan") * lax.axis_size("sub")
    fits = (
        count * 8 == hidden
        and height % 16 == 0
        and (8 * height) % 128 == 0
        and width % 24 == 0
        and width % (4 * rows) == 0
        and height * rows == 192
        and width * count == 192 * rows
    )
    body = shards_direct if fits else shards_general
    return body(pair, chain_len, *params)


def solution(mesh):
    return jax.shard_map(
        shards,
        mesh=mesh,
        in_specs=(
            P(("groups", "row"), ("chan", "sub"), None),
            P("groups"),
            P(),
            P(),
            P(),
            P(),
            P(),
            P(),
            P(),
            P(),
            P(),
            P(),
        ),
        out_specs=P("groups", ("chan", "sub", "row"), None),
        check_vma=False,
    )
```
